32 devices in a mesh: parts: 2 (over x), lag: 8 (over z, y), row: 2 (over core).
Axes of the slice: x: 2, y: 2, z: 4, core: 2. Of those that a mesh axis runs over, the one named last changes fastest.
Arguments:
- history: bfloat16 [16, 32, 64, 256], P('lag', None, 'parts'), parts along dimension 2, may hold values from -6 to 6
- blocks: bfloat16 [8, 2, 112, 256, 256], P('lag', 'row'), may hold values from -0.0234375 to 0.0234375
- block_row: int32 [8, 2, 112], P('lag', 'row'), may hold values from 0 to 15
- block_source: int32 [8, 2, 112], P('lag', 'row'), may hold values from 0 to 31
- block_lag: int32 [8, 2, 112], P('lag', 'row'), may hold values from 0 to 1
- block_count: int32 [8, 2], P('lag', 'row'), may hold values from 56 to 112, as said below
- cluster_perm: int32 [32], replicated, may hold values from 0 to 31, each once
- self_inverse: bfloat16 [32, 256, 256], P('row'), may hold values from -0.375 to 0.375
- pattern: bfloat16 [32, 64, 256], P('row', 'parts'), parts along dimension 1, may hold values from -6 to 6
- waveform: float32 [12, 64], P(None, 'parts'), parts along dimension 1, may hold values from -5 to 5
Outputs:
- new_history: bfloat16 [16, 32, 64, 256], P('lag', None, 'parts'), parts along dimension 2
The draws below stay inside these ranges and needn't reach their ends.
There are 2 independent parts, one for each index of `parts`. The reference program is written for one: setup_inputs(seed, part) draws one part's arguments, and reference() takes and returns one part's arrays. A program takes and returns all parts, laid end to end along the dimension named above; an argument that names none is the same for every part. Nothing has to cross between parts.
Inputs may be any that keep to these rules, and one draw needn't show every extreme that they name: `block_count`: at least half of each device's blocks are used; some device uses all 112.
All inputs are finite; a program needn't handle non-finite values.
Results may differ from the reference program's by a relative error of at most 0.0075.
Values may be sent and summed in bfloat16 or wider, within the bound.
A program may use at most 64 MiB of HBM per device.

```python
import jax
import jax.numpy as jnp
from jax import lax

B = 256
E = 32
CL_DEV = 16
BLK_DEV = 112
LAG_DEV = 2
STEPS = 12
NCL = 32
LAGS = 16
LAG_SHARDS = 8
ROW_SHARDS = 2


def draw_block_count(key, part):
    key = jax.random.fold_in(key, 11)
    first, second = jax.random.split(key)
    counts = jax.random.randint(first, (LAG_SHARDS * ROW_SHARDS,), BLK_DEV // 2, BLK_DEV + 1)
    chosen = jax.random.randint(second, (), 0, LAG_SHARDS * ROW_SHARDS)
    counts = jnp.where(jnp.arange(LAG_SHARDS * ROW_SHARDS) == chosen, BLK_DEV, counts)
    return counts.reshape(LAG_SHARDS, ROW_SHARDS).astype(jnp.int32)


def place_ends(drawn, stream_key, smallest, largest):
    index_at = [jax.random.randint(jax.random.fold_in(stream_key, axis), (), 0, length) for axis, length in enumerate(drawn.shape)]
    longest = drawn.shape.index(max(drawn.shape))
    beside = index_at[:longest] + [(index_at[longest] + 1) % drawn.shape[longest]] + index_at[longest + 1:]
    return drawn.at[tuple(index_at)].set(smallest).at[tuple(beside)].set(largest)


def block_levels(key, shape, cuts, low, largest):
    def one(dim, shards_of):
        steps = jax.random.uniform(jax.random.fold_in(jax.random.fold_in(key, 6), dim), (shards_of,), jnp.float32, low / len(cuts), largest / len(cuts))
        return jnp.repeat(jnp.exp(steps), shape[dim] // shards_of).reshape((-1,) + (1,) * (len(shape) - dim - 1))

    level = one(*cuts[0])
    for cut in cuts[1:]:
        level = level * one(*cut)
    return level


def gaussian(key, dims, spread, most, cuts=(), dtype=jnp.bfloat16):
    values = spread * jax.random.normal(key, dims, jnp.float32)
    if cuts:
        values = values * block_levels(key, dims, cuts, -0.22, 0.18)
    return jnp.clip(values, -most, most).astype(dtype)


def setup_inputs(seed: int = 0, part: int = 0) -> dict:
    key_of = jax.random.split(jax.random.key(seed), 11)
    part_splits = jax.random.split(jax.random.fold_in(key_of[10], part), 11)
    history = gaussian(part_splits[0], (LAGS, NCL, E, B), 1.0, 6.0, ((0, 8),))
    blocks = gaussian(key_of[1], (LAG_SHARDS, ROW_SHARDS, BLK_DEV, B, B), (4 * B * BLK_DEV * LAG_SHARDS // CL_DEV) ** -0.5, 0.0234375, ((0, 8), (1, 2)))
    block_row = place_ends(jax.random.randint(key_of[2], (LAG_SHARDS, ROW_SHARDS, BLK_DEV), 0, CL_DEV), jax.random.fold_in(key_of[2], 1), 0, CL_DEV - 1).astype(jnp.int32)
    block_source = place_ends(jax.random.randint(key_of[3], (LAG_SHARDS, ROW_SHARDS, BLK_DEV), 0, NCL), jax.random.fold_in(key_of[3], 1), 0, NCL - 1).astype(jnp.int32)
    block_lag = place_ends(jax.random.randint(key_of[4], (LAG_SHARDS, ROW_SHARDS, BLK_DEV), 0, LAG_DEV), jax.random.fold_in(key_of[4], 1), 0, LAG_DEV - 1).astype(jnp.int32)
    block_count = draw_block_count(jax.random.fold_in(key_of[10], 71), part)
    cluster_perm = jax.random.permutation(key_of[6], NCL).astype(jnp.int32)
    self_inverse = gaussian(key_of[7], (NCL, B, B), B ** -0.5, 0.375, ((0, 2),))
    pattern = gaussian(part_splits[8], (NCL, E, B), 1.0, 6.0, ((0, 2),))
    waveform = gaussian(part_splits[9], (STEPS, E), 1.0, 5.0, (), jnp.float32)
    return dict(history=history, blocks=blocks, block_row=block_row, block_source=block_source, block_lag=block_lag, block_count=block_count, cluster_perm=cluster_perm, self_inverse=self_inverse, pattern=pattern, waveform=waveform)


def reference(history, blocks, block_row, block_source, block_lag, block_count, cluster_perm, self_inverse, pattern, waveform):
    state = history
    for moment in range(STEPS):
        flattened = state.reshape(LAGS * NCL, E, B)

        def shard_term(total, lag_shard):
            storage = cluster_perm[block_source[lag_shard]]
            positions = ((lag_shard * LAG_DEV + block_lag[lag_shard]) * NCL + storage).astype(jnp.int32)
            selected = flattened[positions].astype(jnp.float32)
            matrices = blocks[lag_shard].astype(jnp.float32)
            products = jnp.einsum("rbes,rbts->rbet", selected, matrices, precision=lax.Precision.HIGHEST)
            usable = jnp.arange(BLK_DEV)[None, :] < block_count[lag_shard][:, None]
            owners = jnp.arange(ROW_SHARDS)[:, None] * CL_DEV + block_row[lag_shard]
            routing = ((owners[:, :, None] == jnp.arange(NCL)[None, None, :]) & usable[:, :, None]).astype(jnp.float32)
            return total + jnp.einsum("rbc,rbet->cet", routing, products, precision=lax.Precision.HIGHEST), None

        lagsum, ignored = lax.scan(shard_term, jnp.zeros((NCL, E, B), jnp.float32), jnp.arange(LAG_SHARDS))
        driven = (waveform[moment][None, :, None] * pattern.astype(jnp.float32) - lagsum).astype(jnp.bfloat16)
        current = jnp.einsum("ces,crs->cer", driven.astype(jnp.float32), self_inverse.astype(jnp.float32), precision=lax.Precision.HIGHEST).astype(jnp.bfloat16)
        state = jnp.concatenate([current[None], state[:-1]], axis=0)
    return state
```

```python
import functools

import jax
import jax.numpy as jnp
from jax import lax
from jax.experimental import pallas as pl
from jax.experimental.pallas import tpu as pltpu
from jax.sharding import PartitionSpec as P

MESH = pl.DeviceIdType.MESH
UNROLL = 8
CHUNK = 4


def plan(block_row, block_source, block_lag, block_count, cluster_perm, rows):
    clusters = cluster_perm.shape[0]
    sources = block_source.reshape(-1)
    count = sources.shape[0]
    lag = block_lag.reshape(-1)
    number = jnp.arange(count, dtype=jnp.int32)
    matches = sources[:, None] == jnp.arange(clusters, dtype=jnp.int32)[None, :]
    storage = jnp.sum(jnp.where(matches, cluster_perm[None, :], 0), axis=1)
    owner = jnp.where(number < block_count.reshape(()), block_row.reshape(-1), rows)
    key = owner * count + number
    rank = jnp.sum((key[None, :] < key[:, None]).astype(jnp.int32), axis=1)
    chosen = rank[None, :] == number[:, None]

    def ordered(values):
        return jnp.sum(jnp.where(chosen, values[None, :], 0), axis=1)

    sorted_owner = ordered(owner)
    even = ordered(((lag + 1) % 2) * clusters + storage)
    odd = ordered((lag % 2) * clusters + storage)
    keep = (
        jnp.concatenate([jnp.full((1,), -1, jnp.int32), sorted_owner[:-1]]) == sorted_owner
    ).astype(jnp.float32)
    members = owner[None, :] == jnp.arange(rows, dtype=jnp.int32)[:, None]
    below = owner[None, :] <= jnp.arange(rows, dtype=jnp.int32)[:, None]
    end = jnp.maximum(jnp.sum(below.astype(jnp.int32), axis=1) - 1, 0)
    filled = jnp.any(members, axis=1).astype(jnp.float32)
    index = jnp.concatenate([ordered(number), even, odd, end])
    return index, jnp.concatenate([keep, filled])


def kernel(
    shards, steps, index, scale, hist, blocks, inverse, pattern, wave, out,
    state, running, entries, child_odd, child_even, outgoing,
    own_recv, sib_recv, odd_recv, even_recv, sib_send, near_send, far_send, sum_send,
):
    count = blocks.shape[0]
    rows, width, depth = pattern.shape
    clusters = hist.shape[1]
    last = steps + 1
    l = lax.axis_index("lag")
    r = lax.axis_index("row")
    even = lax.rem(l, 2) == 0
    half = pl.ds(r * rows, rows)
    sibling = {"row": 1 - r}

    def lag(distance):
        return {"lag": l + distance}

    has_near = l + 1 < shards
    has_far = jnp.logical_and(even, l + 2 < shards)

    barrier = pltpu.get_barrier_semaphore()

    def greet(device):
        pl.semaphore_signal(barrier, inc=1, device_id=device, device_id_type=MESH)

    greet(sibling)
    pl.when(has_near)(lambda: greet(lag(1)))
    pl.when(l >= 1)(lambda: greet(lag(-1)))
    pl.when(has_far)(lambda: greet(lag(2)))
    back = jnp.logical_and(even, l >= 2)
    pl.when(back)(lambda: greet(lag(-2)))
    total = 1
    for flag in (has_near, l >= 1, has_far, back):
        total = total + flag.astype(jnp.int32)
    pl.semaphore_wait(barrier, total)

    def remote(src, dst, send, recv, device):
        return pltpu.make_async_remote_copy(
            src_ref=src, dst_ref=dst, send_sem=send, recv_sem=recv,
            device_id=device, device_id_type=MESH,
        )

    def near(i, src):
        return remote(src, entries.at[i + 2, half], near_send.at[i], own_recv.at[i + 2], lag(1))

    def far(i, src):
        return remote(src, entries.at[i + 4, half], far_send.at[i], own_recv.at[i + 4], lag(2))

    def across(i):
        here = entries.at[i, half]
        return remote(here, here, sib_send.at[i], sib_recv.at[i], sibling)

    def own(i):
        return entries.at[i, half]

    def sum_down(n):
        return (
            remote(outgoing.at[n], child_odd.at[n], sum_send.at[n], odd_recv.at[n], lag(-1)),
            remote(outgoing.at[n], child_even.at[n], sum_send.at[n], even_recv.at[n], lag(-2)),
        )

    for i in range(2):
        pl.when(has_near)(lambda: near(i, hist.at[1 - i, half]).start())
        pl.when(has_far)(lambda: far(i, hist.at[1 - i, half]).start())
        state[i * clusters : (i + 1) * clusters] = hist[1 - i]

    def acquire(i):
        @pl.when(l >= 1)
        def _():
            pltpu.make_async_copy(own(i), own(i), own_recv.at[i]).wait()
            across(i).start()

        pl.when(jnp.logical_and(jnp.logical_and(even, has_near), i + 2 <= last))(
            lambda: near(i, own(i)).start()
        )
        pl.when(jnp.logical_and(has_far, i + 4 <= last))(lambda: far(i, own(i)).start())
        across(i).wait_recv()

    def step(n, carry):
        @pl.when(n >= 1)
        def _():
            acquire(n + 1)
            slot = lax.rem(n + 1, 2) * clusters

            def move(c, _):
                state[slot + c] = entries[n + 1, c]
                return 0

            lax.fori_loop(0, clusters, move, 0)

        places = count + lax.rem(n, 2) * count

        def group(g, held):
            for u in range(UNROLL):
                b = g * UNROLL + u
                product = lax.dot_general(
                    state[index[places + b]], blocks[index[b]], (((1,), (1,)), ((), ())),
                    preferred_element_type=jnp.float32,
                )
                held = held * scale[b] + product
                running[b] = held
            return held

        lax.fori_loop(0, count // UNROLL, group, jnp.zeros((width, depth), jnp.float32))

        def partial(c):
            return running[index[3 * count + c]] * scale[count + c]

        pl.when(jnp.logical_and(even, has_near))(
            lambda: pltpu.make_async_copy(child_odd.at[n], child_odd.at[n], odd_recv.at[n]).wait()
        )
        pl.when(has_far)(
            lambda: pltpu.make_async_copy(child_even.at[n], child_even.at[n], even_recv.at[n]).wait()
        )

        @pl.when(l == 0)
        def _():
            def solve(g, _):
                for u in range(CHUNK):
                    c = g * CHUNK + u
                    lagsum = partial(c) + child_odd[n, c].astype(jnp.float32)
                    if shards > 2:
                        lagsum = lagsum + child_even[n, c].astype(jnp.float32)
                    driven = wave[n] * pattern[c].astype(jnp.float32) - lagsum
                    solved = lax.dot_general(
                        driven.astype(jnp.bfloat16), inverse[c], (((1,), (1,)), ((), ())),
                        preferred_element_type=jnp.float32,
                    )
                    entries[n + 2, r * rows + c] = solved.astype(jnp.bfloat16)
                piece = entries.at[n + 2, pl.ds(r * rows + g * CHUNK, CHUNK)]
                remote(piece, piece, sib_send.at[n + 2], sib_recv.at[n + 2], sibling).start()
                return 0

            lax.fori_loop(0, rows // CHUNK, solve, 0)

        def collect(terms):
            def one(c, _):
                value = partial(c)
                for term in terms:
                    value = value + term[n, c].astype(jnp.float32)
                outgoing[n, c] = value.astype(jnp.bfloat16)
                return 0

            lax.fori_loop(0, rows, one, 0)

        @pl.when(jnp.logical_not(even))
        def _():
            collect(())
            sum_down(n)[0].start()

        @pl.when(back)
        def _():
            pl.when(has_far)(lambda: collect((child_odd, child_even)))
            pl.when(jnp.logical_not(has_far))(lambda: collect((child_odd,)))
            sum_down(n)[1].start()

        return carry

    lax.fori_loop(0, steps, step, 0)
    acquire(last)
    out[0] = entries[last]
    out[1] = entries[last - 1]

    def drain(i, carry):
        pl.when(i >= 2)(lambda: across(i).wait_send())
        pl.when(
            jnp.logical_and(has_near, jnp.logical_or(i < 2, jnp.logical_and(even, i + 2 <= last)))
        )(lambda: near(i, own(i)).wait_send())
        pl.when(jnp.logical_and(has_far, i + 4 <= last))(lambda: far(i, own(i)).wait_send())
        pl.when(jnp.logical_and(l >= 1, i < steps))(lambda: sum_down(i)[0].wait_send())
        return carry

    lax.fori_loop(0, last + 1, drain, 0)


def body(
    shards,
    history,
    blocks,
    block_row,
    block_source,
    block_lag,
    block_count,
    cluster_perm,
    self_inverse,
    pattern,
    waveform,
):
    rows, width, depth = pattern.shape
    steps = waveform.shape[0]
    lags, clusters = history.shape[:2]
    matrices = blocks.reshape(blocks.shape[2:])
    count = matrices.shape[0]
    index, scale = plan(block_row, block_source, block_lag, block_count, cluster_perm, rows)
    wave = jnp.broadcast_to(waveform[:, :, None], (steps, width, depth))
    vmem = pl.BlockSpec(memory_space=pltpu.VMEM)
    smem = pl.BlockSpec(memory_space=pltpu.SMEM)
    slots = steps + lags
    return pl.pallas_call(
        functools.partial(kernel, shards, steps),
        out_shape=jax.ShapeDtypeStruct(history.shape, history.dtype),
        in_specs=[smem, smem] + [vmem] * 5,
        out_specs=vmem,
        scratch_shapes=[
            pltpu.VMEM((lags * clusters, width, depth), jnp.bfloat16),
            pltpu.VMEM((count, width, depth), jnp.float32),
            pltpu.VMEM((slots, clusters, width, depth), jnp.bfloat16),
            pltpu.VMEM((steps, rows, width, depth), jnp.bfloat16),
            pltpu.VMEM((steps, rows, width, depth), jnp.bfloat16),
            pltpu.VMEM((steps, rows, width, depth), jnp.bfloat16),
            pltpu.SemaphoreType.DMA((slots,)),
            pltpu.SemaphoreType.DMA((slots,)),
            pltpu.SemaphoreType.DMA((steps,)),
            pltpu.SemaphoreType.DMA((steps,)),
            pltpu.SemaphoreType.DMA((slots,)),
            pltpu.SemaphoreType.DMA((slots,)),
            pltpu.SemaphoreType.DMA((slots,)),
            pltpu.SemaphoreType.DMA((steps,)),
        ],
        compiler_params=pltpu.CompilerParams(
            collective_id=0, has_side_effects=True, vmem_limit_bytes=58 * 1024 * 1024
        ),
        name="march",
    )(index, scale, history, matrices, self_inverse, pattern, wave)


def solution(mesh):
    in_specs = (
        P("lag", None, "parts", None),
        P("lag", "row", None, None, None),
        P("lag", "row", None),
        P("lag", "row", None),
        P("lag", "row", None),
        P("lag", "row"),
        P(),
        P("row", None, None),
        P("row", "parts", None),
        P(None, "parts"),
    )
    out_specs = P("lag", None, "parts", None)
    return jax.shard_map(
        functools.partial(body, mesh.shape["lag"]), mesh=mesh, in_specs=in_specs,
        out_specs=out_specs, check_vma=False,
    )
```

```python
import functools

import jax
import jax.numpy as jnp
from jax import lax
from jax.experimental import pallas as pl
from jax.experimental.pallas import tpu as pltpu
from jax.sharding import PartitionSpec as P

MESH = pl.DeviceIdType.MESH
UNROLL = 28
CHUNK = 4


def plan(block_row, block_source, block_lag, block_count, cluster_perm, rows):
    clusters = cluster_perm.shape[0]
    sources = block_source.reshape(-1)
    count = sources.shape[0]
    lag = block_lag.reshape(-1)
    number = jnp.arange(count, dtype=jnp.int32)
    matches = sources[:, None] == jnp.arange(clusters, dtype=jnp.int32)[None, :]
    storage = jnp.sum(jnp.where(matches, cluster_perm[None, :], 0), axis=1)
    owner = jnp.where(number < block_count.reshape(()), block_row.reshape(-1), rows)
    key = owner * count + number
    rank = jnp.sum((key[None, :] < key[:, None]).astype(jnp.int32), axis=1)
    chosen = rank[None, :] == number[:, None]

    def ordered(values):
        return jnp.sum(jnp.where(chosen, values[None, :], 0), axis=1)

    sorted_owner = ordered(owner)
    even = ordered(((lag + 1) % 2) * clusters + storage)
    odd = ordered((lag % 2) * clusters + storage)
    keep = (
        jnp.concatenate([jnp.full((1,), -1, jnp.int32), sorted_owner[:-1]]) == sorted_owner
    ).astype(jnp.float32)
    members = owner[None, :] == jnp.arange(rows, dtype=jnp.int32)[:, None]
    below = owner[None, :] <= jnp.arange(rows, dtype=jnp.int32)[:, None]
    end = jnp.maximum(jnp.sum(below.astype(jnp.int32), axis=1) - 1, 0)
    filled = jnp.any(members, axis=1).astype(jnp.float32)
    index = jnp.concatenate([ordered(number), even, odd, end])
    return index, jnp.concatenate([keep, filled])


def kernel(
    shards, steps, index, scale, hist, blocks, inverse, pattern, wave, out,
    state, running, entries, child_odd, child_even, outgoing,
    own_recv, sib_recv, odd_recv, even_recv, sib_send, near_send, far_send, sum_send,
):
    count = blocks.shape[0]
    rows, width, depth = pattern.shape
    clusters = hist.shape[1]
    last = steps + 1
    l = lax.axis_index("lag")
    r = lax.axis_index("row")
    even = lax.rem(l, 2) == 0
    half = pl.ds(r * rows, rows)
    sibling = {"row": 1 - r}

    def lag(distance):
        return {"lag": l + distance}

    has_near = l + 1 < shards
    has_far = jnp.logical_and(even, l + 2 < shards)

    barrier = pltpu.get_barrier_semaphore()

    def greet(device):
        pl.semaphore_signal(barrier, inc=1, device_id=device, device_id_type=MESH)

    greet(sibling)
    pl.when(has_near)(lambda: greet(lag(1)))
    pl.when(l >= 1)(lambda: greet(lag(-1)))
    pl.when(has_far)(lambda: greet(lag(2)))
    back = jnp.logical_and(even, l >= 2)
    pl.when(back)(lambda: greet(lag(-2)))
    total = 1
    for flag in (has_near, l >= 1, has_far, back):
        total = total + flag.astype(jnp.int32)
    pl.semaphore_wait(barrier, total)

    def remote(src, dst, send, recv, device):
        return pltpu.make_async_remote_copy(
            src_ref=src, dst_ref=dst, send_sem=send, recv_sem=recv,
            device_id=device, device_id_type=MESH,
        )

    def near(i, src):
        return remote(src, entries.at[i + 2, half], near_send.at[i], own_recv.at[i + 2], lag(1))

    def far(i, src):
        return remote(src, entries.at[i + 4, half], far_send.at[i], own_recv.at[i + 4], lag(2))

    def across(i):
        here = entries.at[i, half]
        return remote(here, here, sib_send.at[i], sib_recv.at[i], sibling)

    def own(i):
        return entries.at[i, half]

    def sum_down(n, g):
        src = outgoing.at[n, pl.ds(g * CHUNK, CHUNK)]
        sem = sum_send.at[n]
        part = pl.ds(g * CHUNK, CHUNK)
        return (
            lambda: remote(src, child_odd.at[n, part], sem, odd_recv.at[n, g], lag(-1)),
            lambda: remote(src, child_even.at[n, part], sem, even_recv.at[n, g], lag(-2)),
        )

    def await_sums(n, g):
        part = pl.ds(g * CHUNK, CHUNK)

        @pl.when(jnp.logical_and(even, has_near))
        def _():
            ref = child_odd.at[n, part]
            pltpu.make_async_copy(ref, ref, odd_recv.at[n, g]).wait()

        @pl.when(has_far)
        def _():
            ref = child_even.at[n, part]
            pltpu.make_async_copy(ref, ref, even_recv.at[n, g]).wait()

    for i in range(2):
        pl.when(has_near)(lambda: near(i, hist.at[1 - i, half]).start())
        state[i * clusters : (i + 1) * clusters] = hist[1 - i]

    def relay(i):
        @pl.when(l >= 1)
        def _():
            pltpu.make_async_copy(own(i), own(i), own_recv.at[i]).wait()
            across(i).start()

        pl.when(jnp.logical_and(jnp.logical_and(back, has_near), i + 2 <= last))(
            lambda: near(i, own(i)).start()
        )
        pl.when(jnp.logical_and(jnp.logical_and(back, has_far), i + 4 <= last))(
            lambda: far(i, own(i)).start()
        )

    def step(n, carry):
        @pl.when(n >= 1)
        def _():
            @pl.when(n == 1)
            def _():
                for i in range(2):
                    pl.when(has_far)(lambda: far(i, hist.at[1 - i, half]).start())
                pl.when(back)(lambda: relay(2))

            pl.when(back)(lambda: relay(n + 2))
            pl.when(jnp.logical_not(back))(lambda: relay(n + 1))
            across(n + 1).wait_recv()
            slot = lax.rem(n + 1, 2) * clusters

            def move(c, _):
                state[slot + c] = entries[n + 1, c]
                return 0

            lax.fori_loop(0, clusters, move, 0)

        places = count + lax.rem(n, 2) * count

        def group(g, held):
            for u in range(UNROLL):
                b = g * UNROLL + u
                product = lax.dot_general(
                    state[index[places + b]], blocks[index[b]], (((1,), (1,)), ((), ())),
                    preferred_element_type=jnp.float32,
                )
                held = held * scale[b] + product
                running[b] = held
            return held

        lax.fori_loop(0, count // UNROLL, group, jnp.zeros((width, depth), jnp.float32))

        def partial(c):
            return running[index[3 * count + c]] * scale[count + c]

        @pl.when(l == 0)
        def _():
            width_steps = lax.broadcasted_iota(jnp.int32, wave.shape, 1)
            drive = jnp.sum(jnp.where(width_steps == n, wave[...], 0.0), axis=1, keepdims=True)

            def solve(g, _):
                await_sums(n, g)
                for u in range(CHUNK):
                    c = g * CHUNK + u
                    lagsum = partial(c) + child_odd[n, c].astype(jnp.float32)
                    if shards > 2:
                        lagsum = lagsum + child_even[n, c].astype(jnp.float32)
                    driven = drive * pattern[c].astype(jnp.float32) - lagsum
                    solved = lax.dot_general(
                        driven.astype(jnp.bfloat16), inverse[c], (((1,), (1,)), ((), ())),
                        preferred_element_type=jnp.float32,
                    )
                    entries[n + 2, r * rows + c] = solved.astype(jnp.bfloat16)
                piece = entries.at[n + 2, pl.ds(r * rows + g * CHUNK, CHUNK)]
                remote(piece, piece, sib_send.at[n + 2], sib_recv.at[n + 2], sibling).start()
                if shards > 1:

                    @pl.when(n + 4 <= last)
                    def _():
                        there = entries.at[n + 4, pl.ds(r * rows + g * CHUNK, CHUNK)]
                        remote(
                            piece, there, near_send.at[n + 2], own_recv.at[n + 4], lag(1)
                        ).start()

                if shards > 2:

                    @pl.when(n + 6 <= last)
                    def _():
                        there = entries.at[n + 6, pl.ds(r * rows + g * CHUNK, CHUNK)]
                        remote(
                            piece, there, far_send.at[n + 2], own_recv.at[n + 6], lag(2)
                        ).start()

                return 0

            lax.fori_loop(0, rows // CHUNK, solve, 0)

        def collect(terms, target):
            def piece(g, _):
                if terms:
                    await_sums(n, g)
                for u in range(CHUNK):
                    c = g * CHUNK + u
                    value = partial(c)
                    for term in terms:
                        value = value + term[n, c].astype(jnp.float32)
                    outgoing[n, c] = value.astype(jnp.bfloat16)
                sum_down(n, g)[target]().start()
                return 0

            lax.fori_loop(0, rows // CHUNK, piece, 0)

        pl.when(jnp.logical_not(even))(lambda: collect((), 0))

        @pl.when(back)
        def _():
            pl.when(has_far)(lambda: collect((child_odd, child_even), 1))
            pl.when(jnp.logical_not(has_far))(lambda: collect((child_odd,), 1))

        return carry

    lax.fori_loop(0, steps, step, 0)
    pl.when(jnp.logical_not(back))(lambda: relay(last))
    across(last).wait_recv()
    out[0] = entries[last]
    out[1] = entries[last - 1]

    def drain(i, carry):
        pl.when(i >= 2)(lambda: across(i).wait_send())
        pl.when(
            jnp.logical_and(has_near, jnp.logical_or(i < 2, jnp.logical_and(even, i + 2 <= last)))
        )(lambda: near(i, own(i)).wait_send())
        pl.when(jnp.logical_and(has_far, i + 4 <= last))(lambda: far(i, own(i)).wait_send())
        whole = outgoing.at[i]
        pl.when(jnp.logical_and(l >= 1, i < steps))(
            lambda: pltpu.make_async_copy(whole, whole, sum_send.at[i]).wait()
        )
        return carry

    lax.fori_loop(0, last + 1, drain, 0)


def body(
    shards,
    history,
    blocks,
    block_row,
    block_source,
    block_lag,
    block_count,
    cluster_perm,
    self_inverse,
    pattern,
    waveform,
):
    rows, width, depth = pattern.shape
    steps = waveform.shape[0]
    lags, clusters = history.shape[:2]
    matrices = blocks.reshape(blocks.shape[2:])
    count = matrices.shape[0]
    index, scale = plan(block_row, block_source, block_lag, block_count, cluster_perm, rows)
    wave = waveform.T
    vmem = pl.BlockSpec(memory_space=pltpu.VMEM)
    smem = pl.BlockSpec(memory_space=pltpu.SMEM)
    slots = steps + lags
    return pl.pallas_call(
        functools.partial(kernel, shards, steps),
        out_shape=jax.ShapeDtypeStruct(history.shape, history.dtype),
        in_specs=[smem, smem] + [vmem] * 5,
        out_specs=vmem,
        scratch_shapes=[
            pltpu.VMEM((lags * clusters, width, depth), jnp.bfloat16),
            pltpu.VMEM((count, width, depth), jnp.float32),
            pltpu.VMEM((slots, clusters, width, depth), jnp.bfloat16),
            pltpu.VMEM((steps, rows, width, depth), jnp.bfloat16),
            pltpu.VMEM((steps, rows, width, depth), jnp.bfloat16),
            pltpu.VMEM((steps, rows, width, depth), jnp.bfloat16),
            pltpu.SemaphoreType.DMA((slots,)),
            pltpu.SemaphoreType.DMA((slots,)),
            pltpu.SemaphoreType.DMA((steps, rows // CHUNK)),
            pltpu.SemaphoreType.DMA((steps, rows // CHUNK)),
            pltpu.SemaphoreType.DMA((slots,)),
            pltpu.SemaphoreType.DMA((slots,)),
            pltpu.SemaphoreType.DMA((slots,)),
            pltpu.SemaphoreType.DMA((steps,)),
        ],
        compiler_params=pltpu.CompilerParams(
            collective_id=0, has_side_effects=True, vmem_limit_bytes=58 * 1024 * 1024
        ),
        name="march",
    )(index, scale, history, matrices, self_inverse, pattern, wave)


def solution(mesh):
    in_specs = (
        P("lag", None, "parts", None),
        P("lag", "row", None, None, None),
        P("lag", "row", None),
        P("lag", "row", None),
        P("lag", "row", None),
        P("lag", "row"),
        P(),
        P("row", None, None),
        P("row", "parts", None),
        P(None, "parts"),
    )
    out_specs = P("lag", None, "parts", None)
    return jax.shard_map(
        functools.partial(body, mesh.shape["lag"]), mesh=mesh, in_specs=in_specs,
        out_specs=out_specs, check_vma=False,
    )
```

```python
import functools

import jax
import jax.numpy as jnp
from jax import lax
from jax.experimental import pallas as pl
from jax.experimental.pallas import tpu as pltpu
from jax.sharding import PartitionSpec as P

MESH = pl.DeviceIdType.MESH
UNROLL = 28
CHUNK = 4


def plan(block_row, block_source, block_lag, block_count, cluster_perm, rows):
    clusters = cluster_perm.shape[0]
    sources = block_source.reshape(-1)
    count = sources.shape[0]
    lag = block_lag.reshape(-1)
    number = jnp.arange(count, dtype=jnp.int32)
    matches = sources[:, None] == jnp.arange(clusters, dtype=jnp.int32)[None, :]
    storage = jnp.sum(jnp.where(matches, cluster_perm[None, :], 0), axis=1)
    owner = jnp.where(number < block_count.reshape(()), block_row.reshape(-1), rows)
    key = owner * count + number
    rank = jnp.sum((key[None, :] < key[:, None]).astype(jnp.int32), axis=1)
    chosen = rank[None, :] == number[:, None]

    def ordered(values):
        return jnp.sum(jnp.where(chosen, values[None, :], 0), axis=1)

    sorted_owner = ordered(owner)
    even = ordered(((lag + 1) % 2) * clusters + storage)
    odd = ordered((lag % 2) * clusters + storage)
    keep = (
        jnp.concatenate([jnp.full((1,), -1, jnp.int32), sorted_owner[:-1]]) == sorted_owner
    ).astype(jnp.float32)
    members = owner[None, :] == jnp.arange(rows, dtype=jnp.int32)[:, None]
    below = owner[None, :] <= jnp.arange(rows, dtype=jnp.int32)[:, None]
    end = jnp.maximum(jnp.sum(below.astype(jnp.int32), axis=1) - 1, 0)
    filled = jnp.any(members, axis=1).astype(jnp.float32)
    index = jnp.concatenate([ordered(number), even, odd, end])
    return index, jnp.concatenate([keep, filled])


def kernel(
    shards, steps, index, scale, hist, blocks, inverse, pattern, wave, out,
    state, running, flipped, flipped_inverse, entries, child_odd, child_even, outgoing,
    own_recv, sib_recv, odd_recv, even_recv, sib_send, near_send, far_send, sum_send,
):
    count = blocks.shape[0]
    rows, width, depth = pattern.shape
    clusters = hist.shape[1]
    last = steps + 1
    l = lax.axis_index("lag")
    r = lax.axis_index("row")
    even = lax.rem(l, 2) == 0
    half = pl.ds(r * rows, rows)
    sibling = {"row": 1 - r}

    def lag(distance):
        return {"lag": l + distance}

    has_near = l + 1 < shards
    has_far = jnp.logical_and(even, l + 2 < shards)

    barrier = pltpu.get_barrier_semaphore()

    def greet(device):
        pl.semaphore_signal(barrier, inc=1, device_id=device, device_id_type=MESH)

    greet(sibling)
    pl.when(has_near)(lambda: greet(lag(1)))
    pl.when(l >= 1)(lambda: greet(lag(-1)))
    pl.when(has_far)(lambda: greet(lag(2)))
    back = jnp.logical_and(even, l >= 2)
    pl.when(back)(lambda: greet(lag(-2)))
    total = 1
    for flag in (has_near, l >= 1, has_far, back):
        total = total + flag.astype(jnp.int32)
    pl.semaphore_wait(barrier, total)

    def remote(src, dst, send, recv, device):
        return pltpu.make_async_remote_copy(
            src_ref=src, dst_ref=dst, send_sem=send, recv_sem=recv,
            device_id=device, device_id_type=MESH,
        )

    def near(i, src):
        return remote(src, entries.at[i + 2, half], near_send.at[i], own_recv.at[i + 2], lag(1))

    def far(i, src):
        return remote(src, entries.at[i + 4, half], far_send.at[i], own_recv.at[i + 4], lag(2))

    def across(i):
        here = entries.at[i, half]
        return remote(here, here, sib_send.at[i], sib_recv.at[i], sibling)

    def own(i):
        return entries.at[i, half]

    def sum_down(n, g):
        src = outgoing.at[n, pl.ds(g * CHUNK, CHUNK)]
        sem = sum_send.at[n]
        part = pl.ds(g * CHUNK, CHUNK)
        return (
            lambda: remote(src, child_odd.at[n, part], sem, odd_recv.at[n, g], lag(-1)),
            lambda: remote(src, child_even.at[n, part], sem, even_recv.at[n, g], lag(-2)),
        )

    def await_sums(n, g):
        part = pl.ds(g * CHUNK, CHUNK)

        @pl.when(jnp.logical_and(even, has_near))
        def _():
            ref = child_odd.at[n, part]
            pltpu.make_async_copy(ref, ref, odd_recv.at[n, g]).wait()

        @pl.when(has_far)
        def _():
            ref = child_even.at[n, part]
            pltpu.make_async_copy(ref, ref, even_recv.at[n, g]).wait()

    for i in range(2):
        pl.when(has_near)(lambda: near(i, hist.at[1 - i, half]).start())
        state[i * clusters : (i + 1) * clusters] = hist[1 - i]

    def relay(i):
        @pl.when(l >= 1)
        def _():
            pltpu.make_async_copy(own(i), own(i), own_recv.at[i]).wait()
            across(i).start()

        pl.when(jnp.logical_and(jnp.logical_and(back, has_near), i + 2 <= last))(
            lambda: near(i, own(i)).start()
        )
        pl.when(jnp.logical_and(jnp.logical_and(back, has_far), i + 4 <= last))(
            lambda: far(i, own(i)).start()
        )

    def step(n, carry):
        @pl.when(n >= 1)
        def _():
            @pl.when(n == 1)
            def _():
                for i in range(2):
                    pl.when(has_far)(lambda: far(i, hist.at[1 - i, half]).start())
                pl.when(back)(lambda: relay(2))

            pl.when(back)(lambda: relay(n + 2))
            pl.when(jnp.logical_not(back))(lambda: relay(n + 1))
            across(n + 1).wait_recv()
            slot = lax.rem(n + 1, 2) * clusters

            def move(c, _):
                state[slot + c] = entries[n + 1, c]
                return 0

            lax.fori_loop(0, clusters, move, 0)

        places = count + lax.rem(n, 2) * count

        def group(first, g, held):
            for u in range(UNROLL):
                b = g * UNROLL + u
                if first:
                    turned = blocks[index[b]].T
                    flipped[b] = turned
                else:
                    turned = flipped[b]
                product = jnp.dot(
                    state[index[places + b]], turned, preferred_element_type=jnp.float32
                )
                held = held * scale[b] + product
                running[b] = held
            return held

        def multiply(first):
            zero = jnp.zeros((width, depth), jnp.float32)
            lax.fori_loop(0, count // UNROLL, functools.partial(group, first), zero)

        pl.when(n == 0)(lambda: multiply(True))
        pl.when(n > 0)(lambda: multiply(False))

        @pl.when(jnp.logical_and(n == 0, l == 0))
        def _():
            def turn(c, _):
                flipped_inverse[c] = inverse[c].T
                return 0

            lax.fori_loop(0, rows, turn, 0)

        def partial(c):
            return running[index[3 * count + c]] * scale[count + c]

        @pl.when(l == 0)
        def _():
            width_steps = lax.broadcasted_iota(jnp.int32, wave.shape, 1)
            drive = jnp.sum(jnp.where(width_steps == n, wave[...], 0.0), axis=1, keepdims=True)

            def solve(g, _):
                await_sums(n, g)
                for u in range(CHUNK):
                    c = g * CHUNK + u
                    lagsum = partial(c) + child_odd[n, c].astype(jnp.float32)
                    if shards > 2:
                        lagsum = lagsum + child_even[n, c].astype(jnp.float32)
                    driven = drive * pattern[c].astype(jnp.float32) - lagsum
                    solved = jnp.dot(
                        driven.astype(jnp.bfloat16), flipped_inverse[c],
                        preferred_element_type=jnp.float32,
                    )
                    entries[n + 2, r * rows + c] = solved.astype(jnp.bfloat16)
                piece = entries.at[n + 2, pl.ds(r * rows + g * CHUNK, CHUNK)]
                remote(piece, piece, sib_send.at[n + 2], sib_recv.at[n + 2], sibling).start()
                if shards > 1:

                    @pl.when(n + 4 <= last)
                    def _():
                        there = entries.at[n + 4, pl.ds(r * rows + g * CHUNK, CHUNK)]
                        remote(
                            piece, there, near_send.at[n + 2], own_recv.at[n + 4], lag(1)
                        ).start()

                if shards > 2:

                    @pl.when(n + 6 <= last)
                    def _():
                        there = entries.at[n + 6, pl.ds(r * rows + g * CHUNK, CHUNK)]
                        remote(
                            piece, there, far_send.at[n + 2], own_recv.at[n + 6], lag(2)
                        ).start()

                return 0

            lax.fori_loop(0, rows // CHUNK, solve, 0)

        def collect(terms, target):
            def piece(g, _):
                if terms:
                    await_sums(n, g)
                for u in range(CHUNK):
                    c = g * CHUNK + u
                    value = partial(c)
                    for term in terms:
                        value = value + term[n, c].astype(jnp.float32)
                    outgoing[n, c] = value.astype(jnp.bfloat16)
                sum_down(n, g)[target]().start()
                return 0

            lax.fori_loop(0, rows // CHUNK, piece, 0)

        pl.when(jnp.logical_not(even))(lambda: collect((), 0))

        @pl.when(back)
        def _():
            pl.when(has_far)(lambda: collect((child_odd, child_even), 1))
            pl.when(jnp.logical_not(has_far))(lambda: collect((child_odd,), 1))

        return carry

    lax.fori_loop(0, steps, step, 0)
    pl.when(jnp.logical_not(back))(lambda: relay(last))
    across(last).wait_recv()
    out[0] = entries[last]
    out[1] = entries[last - 1]

    def drain(i, carry):
        pl.when(i >= 2)(lambda: across(i).wait_send())
        pl.when(
            jnp.logical_and(has_near, jnp.logical_or(i < 2, jnp.logical_and(even, i + 2 <= last)))
        )(lambda: near(i, own(i)).wait_send())
        pl.when(jnp.logical_and(has_far, i + 4 <= last))(lambda: far(i, own(i)).wait_send())
        whole = outgoing.at[i]
        pl.when(jnp.logical_and(l >= 1, i < steps))(
            lambda: pltpu.make_async_copy(whole, whole, sum_send.at[i]).wait()
        )
        return carry

    lax.fori_loop(0, last + 1, drain, 0)


def body(
    shards,
    history,
    blocks,
    block_row,
    block_source,
    block_lag,
    block_count,
    cluster_perm,
    self_inverse,
    pattern,
    waveform,
):
    rows, width, depth = pattern.shape
    steps = waveform.shape[0]
    lags, clusters = history.shape[:2]
    matrices = blocks.reshape(blocks.shape[2:])
    count = matrices.shape[0]
    index, scale = plan(block_row, block_source, block_lag, block_count, cluster_perm, rows)
    wave = waveform.T
    vmem = pl.BlockSpec(memory_space=pltpu.VMEM)
    smem = pl.BlockSpec(memory_space=pltpu.SMEM)
    slots = steps + lags
    return pl.pallas_call(
        functools.partial(kernel, shards, steps),
        out_shape=jax.ShapeDtypeStruct(history.shape, history.dtype),
        in_specs=[smem, smem] + [vmem] * 5,
        out_specs=vmem,
        scratch_shapes=[
            pltpu.VMEM((lags * clusters, width, depth), jnp.bfloat16),
            pltpu.VMEM((count, width, depth), jnp.float32),
            pltpu.VMEM((count, depth, depth), jnp.bfloat16),
            pltpu.VMEM((rows, depth, depth), jnp.bfloat16),
            pltpu.VMEM((slots, clusters, width, depth), jnp.bfloat16),
            pltpu.VMEM((steps, rows, width, depth), jnp.bfloat16),
            pltpu.VMEM((steps, rows, width, depth), jnp.bfloat16),
            pltpu.VMEM((steps, rows, width, depth), jnp.bfloat16),
            pltpu.SemaphoreType.DMA((slots,)),
            pltpu.SemaphoreType.DMA((slots,)),
            pltpu.SemaphoreType.DMA((steps, rows // CHUNK)),
            pltpu.SemaphoreType.DMA((steps, rows // CHUNK)),
            pltpu.SemaphoreType.DMA((slots,)),
            pltpu.SemaphoreType.DMA((slots,)),
            pltpu.SemaphoreType.DMA((slots,)),
            pltpu.SemaphoreType.DMA((steps,)),
        ],
        compiler_params=pltpu.CompilerParams(
            collective_id=0, has_side_effects=True, vmem_limit_bytes=60 * 1024 * 1024
        ),
        name="march",
    )(index, scale, history, matrices, self_inverse, pattern, wave)


def solution(mesh):
    in_specs = (
        P("lag", None, "parts", None),
        P("lag", "row", None, None, None),
        P("lag", "row", None),
        P("lag", "row", None),
        P("lag", "row", None),
        P("lag", "row"),
        P(),
        P("row", None, None),
        P("row", "parts", None),
        P(None, "parts"),
    )
    out_specs = P("lag", None, "parts", None)
    return jax.shard_map(
        functools.partial(body, mesh.shape["lag"]), mesh=mesh, in_specs=in_specs,
        out_specs=out_specs, check_vma=False,
    )
```

```python
import functools

import jax
import jax.numpy as jnp
from jax import lax
from jax.experimental import pallas as pl
from jax.experimental.pallas import tpu as pltpu
from jax.sharding import PartitionSpec as P

MESH = pl.DeviceIdType.MESH
UNROLL = 56
CHUNK = 4


def plan(block_row, block_source, block_lag, block_count, cluster_perm, rows):
    clusters = cluster_perm.shape[0]
    sources = block_source.reshape(-1)
    count = sources.shape[0]
    lag = block_lag.reshape(-1)
    number = jnp.arange(count, dtype=jnp.int32)
    matches = sources[:, None] == jnp.arange(clusters, dtype=jnp.int32)[None, :]
    storage = jnp.sum(jnp.where(matches, cluster_perm[None, :], 0), axis=1)
    owner = jnp.where(number < block_count.reshape(()), block_row.reshape(-1), rows)
    key = owner * count + number
    rank = jnp.sum((key[None, :] < key[:, None]).astype(jnp.int32), axis=1)
    chosen = rank[None, :] == number[:, None]

    def ordered(values):
        return jnp.sum(jnp.where(chosen, values[None, :], 0), axis=1)

    sorted_owner = ordered(owner)
    even = ordered(((lag + 1) % 2) * clusters + storage)
    odd = ordered((lag % 2) * clusters + storage)
    keep = (
        jnp.concatenate([jnp.full((1,), -1, jnp.int32), sorted_owner[:-1]]) == sorted_owner
    ).astype(jnp.float32)
    members = owner[None, :] == jnp.arange(rows, dtype=jnp.int32)[:, None]
    below = owner[None, :] <= jnp.arange(rows, dtype=jnp.int32)[:, None]
    end = jnp.maximum(jnp.sum(below.astype(jnp.int32), axis=1) - 1, 0)
    filled = jnp.any(members, axis=1).astype(jnp.float32)
    index = jnp.concatenate([ordered(number), even, odd, end])
    return index, jnp.concatenate([keep, filled])


def kernel(
    shards, steps, index, scale, hist, blocks, inverse, pattern, wave, out,
    state, running, flipped, flipped_inverse, entries, child_odd, child_even, outgoing,
    own_recv, sib_recv, odd_recv, even_recv, sib_send, near_send, far_send, sum_send,
):
    count = blocks.shape[0]
    rows, width, depth = pattern.shape
    clusters = hist.shape[1]
    last = steps + 1
    l = lax.axis_index("lag")
    r = lax.axis_index("row")
    even = lax.rem(l, 2) == 0
    half = pl.ds(r * rows, rows)
    sibling = {"row": 1 - r}

    def lag(distance):
        return {"lag": l + distance}

    has_near = l + 1 < shards
    has_far = jnp.logical_and(even, l + 2 < shards)

    barrier = pltpu.get_barrier_semaphore()

    def greet(device):
        pl.semaphore_signal(barrier, inc=1, device_id=device, device_id_type=MESH)

    greet(sibling)
    pl.when(has_near)(lambda: greet(lag(1)))
    pl.when(l >= 1)(lambda: greet(lag(-1)))
    pl.when(has_far)(lambda: greet(lag(2)))
    back = jnp.logical_and(even, l >= 2)
    pl.when(back)(lambda: greet(lag(-2)))
    total = 1
    for flag in (has_near, l >= 1, has_far, back):
        total = total + flag.astype(jnp.int32)
    pl.semaphore_wait(barrier, total)

    def remote(src, dst, send, recv, device):
        return pltpu.make_async_remote_copy(
            src_ref=src, dst_ref=dst, send_sem=send, recv_sem=recv,
            device_id=device, device_id_type=MESH,
        )

    def near(i, src):
        return remote(src, entries.at[i + 2, half], near_send.at[i], own_recv.at[i + 2], lag(1))

    def far(i, src):
        return remote(src, entries.at[i + 4, half], far_send.at[i], own_recv.at[i + 4], lag(2))

    def across(i):
        here = entries.at[i, half]
        return remote(here, here, sib_send.at[i], sib_recv.at[i], sibling)

    def own(i):
        return entries.at[i, half]

    def sum_down(n, g):
        src = outgoing.at[n, pl.ds(g * CHUNK, CHUNK)]
        sem = sum_send.at[n]
        part = pl.ds(g * CHUNK, CHUNK)
        return (
            lambda: remote(src, child_odd.at[n, part], sem, odd_recv.at[n, g], lag(-1)),
            lambda: remote(src, child_even.at[n, part], sem, even_recv.at[n, g], lag(-2)),
        )

    def await_sums(n, g):
        part = pl.ds(g * CHUNK, CHUNK)

        @pl.when(jnp.logical_and(even, has_near))
        def _():
            ref = child_odd.at[n, part]
            pltpu.make_async_copy(ref, ref, odd_recv.at[n, g]).wait()

        @pl.when(has_far)
        def _():
            ref = child_even.at[n, part]
            pltpu.make_async_copy(ref, ref, even_recv.at[n, g]).wait()

    for i in range(2):
        pl.when(has_near)(lambda: near(i, hist.at[1 - i, half]).start())
        state[i * clusters : (i + 1) * clusters] = hist[1 - i]

    def relay(i):
        @pl.when(l >= 1)
        def _():
            pltpu.make_async_copy(own(i), own(i), own_recv.at[i]).wait()
            across(i).start()

        pl.when(jnp.logical_and(jnp.logical_and(back, has_near), i + 2 <= last))(
            lambda: near(i, own(i)).start()
        )
        pl.when(jnp.logical_and(jnp.logical_and(back, has_far), i + 4 <= last))(
            lambda: far(i, own(i)).start()
        )

    def step(n, carry):
        @pl.when(n >= 1)
        def _():
            @pl.when(n == 1)
            def _():
                for i in range(2):
                    pl.when(has_far)(lambda: far(i, hist.at[1 - i, half]).start())
                pl.when(back)(lambda: relay(2))

            pl.when(back)(lambda: relay(n + 2))
            pl.when(jnp.logical_not(back))(lambda: relay(n + 1))
            across(n + 1).wait_recv()
            slot = lax.rem(n + 1, 2) * clusters

            def move(c, _):
                state[slot + c] = entries[n + 1, c]
                return 0

            lax.fori_loop(0, clusters, move, 0)

        places = count + lax.rem(n, 2) * count

        def group(first, g, held):
            for u in range(UNROLL):
                b = g * UNROLL + u
                if first:
                    turned = blocks[index[b]].T
                    flipped[b] = turned
                else:
                    turned = flipped[b]
                product = jnp.dot(
                    state[index[places + b]], turned, preferred_element_type=jnp.float32
                )
                held = held * scale[b] + product
                running[b] = held
            return held

        def multiply(first):
            zero = jnp.zeros((width, depth), jnp.float32)
            lax.fori_loop(0, count // UNROLL, functools.partial(group, first), zero)

        pl.when(n == 0)(lambda: multiply(True))
        pl.when(n > 0)(lambda: multiply(False))

        @pl.when(jnp.logical_and(n == 0, l == 0))
        def _():
            def turn(c, _):
                flipped_inverse[c] = inverse[c].T
                return 0

            lax.fori_loop(0, rows, turn, 0)

        def partial(c):
            return running[index[3 * count + c]] * scale[count + c]

        @pl.when(l == 0)
        def _():
            width_steps = lax.broadcasted_iota(jnp.int32, wave.shape, 1)
            drive = jnp.sum(jnp.where(width_steps == n, wave[...], 0.0), axis=1, keepdims=True)

            def solve(g, _):
                await_sums(n, g)
                for u in range(CHUNK):
                    c = g * CHUNK + u
                    lagsum = partial(c) + child_odd[n, c].astype(jnp.float32)
                    if shards > 2:
                        lagsum = lagsum + child_even[n, c].astype(jnp.float32)
                    driven = drive * pattern[c].astype(jnp.float32) - lagsum
                    solved = jnp.dot(
                        driven.astype(jnp.bfloat16), flipped_inverse[c],
                        preferred_element_type=jnp.float32,
                    )
                    entries[n + 2, r * rows + c] = solved.astype(jnp.bfloat16)
                piece = entries.at[n + 2, pl.ds(r * rows + g * CHUNK, CHUNK)]
                remote(piece, piece, sib_send.at[n + 2], sib_recv.at[n + 2], sibling).start()
                if shards > 1:

                    @pl.when(n + 4 <= last)
                    def _():
                        there = entries.at[n + 4, pl.ds(r * rows + g * CHUNK, CHUNK)]
                        remote(
                            piece, there, near_send.at[n + 2], own_recv.at[n + 4], lag(1)
                        ).start()

                if shards > 2:

                    @pl.when(n + 6 <= last)
                    def _():
                        there = entries.at[n + 6, pl.ds(r * rows + g * CHUNK, CHUNK)]
                        remote(
                            piece, there, far_send.at[n + 2], own_recv.at[n + 6], lag(2)
                        ).start()

                return 0

            lax.fori_loop(0, rows // CHUNK, solve, 0)

        def collect(terms, target):
            def piece(g, _):
                if terms:
                    await_sums(n, g)
                for u in range(CHUNK):
                    c = g * CHUNK + u
                    value = partial(c)
                    for term in terms:
                        value = value + term[n, c].astype(jnp.float32)
                    outgoing[n, c] = value.astype(jnp.bfloat16)
                sum_down(n, g)[target]().start()
                return 0

            lax.fori_loop(0, rows // CHUNK, piece, 0)

        pl.when(jnp.logical_not(even))(lambda: collect((), 0))

        @pl.when(back)
        def _():
            pl.when(has_far)(lambda: collect((child_odd, child_even), 1))
            pl.when(jnp.logical_not(has_far))(lambda: collect((child_odd,), 1))

        return carry

    lax.fori_loop(0, steps, step, 0)
    pl.when(jnp.logical_not(back))(lambda: relay(last))
    across(last).wait_recv()
    out[0] = entries[last]
    out[1] = entries[last - 1]

    def drain(i, carry):
        pl.when(i >= 2)(lambda: across(i).wait_send())
        pl.when(
            jnp.logical_and(has_near, jnp.logical_or(i < 2, jnp.logical_and(even, i + 2 <= last)))
        )(lambda: near(i, own(i)).wait_send())
        pl.when(jnp.logical_and(has_far, i + 4 <= last))(lambda: far(i, own(i)).wait_send())
        whole = outgoing.at[i]
        pl.when(jnp.logical_and(l >= 1, i < steps))(
            lambda: pltpu.make_async_copy(whole, whole, sum_send.at[i]).wait()
        )
        return carry

    lax.fori_loop(0, last + 1, drain, 0)


def body(
    shards,
    history,
    blocks,
    block_row,
    block_source,
    block_lag,
    block_count,
    cluster_perm,
    self_inverse,
    pattern,
    waveform,
):
    rows, width, depth = pattern.shape
    steps = waveform.shape[0]
    lags, clusters = history.shape[:2]
    matrices = blocks.reshape(blocks.shape[2:])
    count = matrices.shape[0]
    index, scale = plan(block_row, block_source, block_lag, block_count, cluster_perm, rows)
    wave = waveform.T
    vmem = pl.BlockSpec(memory_space=pltpu.VMEM)
    smem = pl.BlockSpec(memory_space=pltpu.SMEM)
    slots = steps + lags
    return pl.pallas_call(
        functools.partial(kernel, shards, steps),
        out_shape=jax.ShapeDtypeStruct(history.shape, history.dtype),
        in_specs=[smem, smem] + [vmem] * 5,
        out_specs=vmem,
        scratch_shapes=[
            pltpu.VMEM((lags * clusters, width, depth), jnp.bfloat16),
            pltpu.VMEM((count, width, depth), jnp.float32),
            pltpu.VMEM((count, depth, depth), jnp.bfloat16),
            pltpu.VMEM((rows, depth, depth), jnp.bfloat16),
            pltpu.VMEM((slots, clusters, width, depth), jnp.bfloat16),
            pltpu.VMEM((steps, rows, width, depth), jnp.bfloat16),
            pltpu.VMEM((steps, rows, width, depth), jnp.bfloat16),
            pltpu.VMEM((steps, rows, width, depth), jnp.bfloat16),
            pltpu.SemaphoreType.DMA((slots,)),
            pltpu.SemaphoreType.DMA((slots,)),
            pltpu.SemaphoreType.DMA((steps, rows // CHUNK)),
            pltpu.SemaphoreType.DMA((steps, rows // CHUNK)),
            pltpu.SemaphoreType.DMA((slots,)),
            pltpu.SemaphoreType.DMA((slots,)),
            pltpu.SemaphoreType.DMA((slots,)),
            pltpu.SemaphoreType.DMA((steps,)),
        ],
        compiler_params=pltpu.CompilerParams(
            collective_id=0, has_side_effects=True, vmem_limit_bytes=60 * 1024 * 1024
        ),
        name="march",
    )(index, scale, history, matrices, self_inverse, pattern, wave)


def solution(mesh):
    in_specs = (
        P("lag", None, "parts", None),
        P("lag", "row", None, None, None),
        P("lag", "row", None),
        P("lag", "row", None),
        P("lag", "row", None),
        P("lag", "row"),
        P(),
        P("row", None, None),
        P("row", "parts", None),
        P(None, "parts"),
    )
    out_specs = P("lag", None, "parts", None)
    return jax.shard_map(
        functools.partial(body, mesh.shape["lag"]), mesh=mesh, in_specs=in_specs,
        out_specs=out_specs, check_vma=False,
    )
```
